32 devices in a mesh: groups: 1, ep: 32 (over z, y, x, core).
Axes of the slice: x: 2, y: 2, z: 4, core: 2. Of those that a mesh axis runs over, the one named last changes fastest.
Arguments:
- queries: bfloat16 [512, 4096], P(('groups', 'ep')), may hold values from -6 to 6
- keys: bfloat16 [512, 192, 256], P(('groups', 'ep')), may hold values from -6 to 6
- values: bfloat16 [512, 192, 256], P(('groups', 'ep')), may hold values from -6 to 6
- kv_lengths: int32 [512], P(('groups', 'ep')), may hold values from 2 to 192
- residual: bfloat16 [512, 4096], P(('groups', 'ep')), may hold values from -6 to 6
- norm_gain: bfloat16 [4096], replicated, may hold values from 0.5 to 1.5
- routes: int32 [512, 8], P(('groups', 'ep')), may hold values from 0 to 15, all different within a row; in each aligned block of 8 rows (0 to 7, 8 to 15, ...) at most 8 rows name the same one
- route_weights: bfloat16 [512, 8], P(('groups', 'ep')), may hold values from 0.099609375 to 0.5
- gate_weight: bfloat16 [32, 4096, 384], P('ep'), may hold values from -0.09375 to 0.09375
- up_weight: bfloat16 [32, 4096, 384], P('ep'), may hold values from -0.09375 to 0.09375
- down_weight: bfloat16 [32, 384, 4096], P('ep'), may hold values from -0.21875 to 0.21875
Outputs:
- layer_out: bfloat16 [512, 4096], P(('groups', 'ep'))
The draws below stay inside these ranges and needn't reach their ends.
Inputs may be any that keep to these rules, and one draw needn't show every extreme that they name: `routes`: in each aligned block of 8 rows no expert is named by more than 8 rows.
All inputs are finite; a program needn't handle non-finite values.
Results may differ from the reference program's by a relative error of at most 0.0075.
Values may be sent and summed in bfloat16 or wider, within the bound.
A program may use at most 128 MiB of HBM per device.

```python
import math
import jax
import jax.numpy as jnp
import numpy as np
from jax import lax

D = 4096
HEADS = 32
KVH = 2
HDIM = 128
HID = 768
TOP = 8
MB_ROWS = 8
CTX = 192
HALF = 384
EXPERTS = 16
CAP = 8
TOKENS = 512
N_EP = 32


def draw_queries(key, part):
    key = jax.random.fold_in(key, 11)
    return jax.random.truncated_normal(key, -4.0, 4.0, (TOKENS, HEADS * HDIM), jnp.float32).astype(jnp.bfloat16)


def draw_keys(key, part):
    key = jax.random.fold_in(key, 12)
    return jax.random.truncated_normal(key, -4.0, 4.0, (TOKENS, CTX, KVH * HDIM), jnp.float32).astype(jnp.bfloat16)


def draw_kv_lengths(key, part):
    key = jax.random.fold_in(key, 13)
    first_key, second_key = jax.random.split(key)
    first_draw = jax.random.randint(first_key, (TOKENS,), 0, CTX - 1, jnp.int32)
    second_draw = jax.random.randint(second_key, (TOKENS,), 0, CTX - 1, jnp.int32)
    lengths = first_draw * second_draw // (CTX - 2) + 2
    row_ids = jnp.arange(TOKENS, dtype=jnp.int32)
    lengths = jnp.where(row_ids == 3, CTX, lengths)
    lengths = jnp.where(row_ids == 5, 2, lengths)
    return lengths.astype(jnp.int32)


def levels(stream_key, dims, pieces, low, largest):
    loudness, own = 1.0, jax.random.fold_in(stream_key, 6)
    for dim, parts in pieces:
        steps = jnp.exp(jax.random.uniform(jax.random.fold_in(own, dim), (parts,), jnp.float32, low / len(pieces), largest / len(pieces)))
        loudness = loudness * jnp.repeat(steps, dims[dim] // parts).reshape([-1 if axis == dim else 1 for axis in range(len(dims))])
    return loudness


def assign_block(key, own, number, rows, amount, top, reach, lean):
    ranking = jax.random.permutation(key, amount)
    crowded, common = load_shares(amount, rows * top, reach, lean, True), load_shares(amount, rows * top, reach, lean, False)
    places = jnp.arange(amount)

    def named(sizes, rotation):
        used = int((sizes > 0).sum())
        fixed = max(1, used // 4)
        passed = fixed + (places - fixed + rotation * (used - fixed)) % max(1, amount - fixed)
        return jnp.zeros((amount,), jnp.int32).at[ranking[jnp.where(places < fixed, places, passed)]].set(jnp.asarray(sizes, jnp.int32))

    sizes = jnp.where(number % 4 == 0, named(crowded, number // 4), named(common, number - number // 4 - 1))
    mixed = jax.random.permutation(jax.random.fold_in(own, 3), amount)
    source_of, taker = mixed[0:amount // 2 * 2:2], mixed[1:amount // 2 * 2:2]
    room = jnp.minimum(sizes[source_of] - 1, reach - sizes[taker]) // 2
    room = jnp.where((source_of == ranking[0]) | (taker == ranking[0]) | (sizes[taker] == 0), 0, jnp.maximum(room, 0))
    passed = jax.random.randint(jax.random.fold_in(own, 4), (amount // 2,), 0, 1 << 20) % (room + 1)
    sizes = sizes.at[source_of].add(-passed).at[taker].add(passed)
    items = jnp.searchsorted(jnp.cumsum(sizes), jnp.arange(rows * top), side="right").astype(jnp.int32)
    table = items.reshape(top, rows).T
    table = table[jax.random.permutation(jax.random.fold_in(own, 1), rows)]
    rotation = jax.random.randint(jax.random.fold_in(own, 2), (rows, 1), 0, top)
    return jnp.take_along_axis(table, (jnp.arange(top)[None, :] + rotation) % top, axis=1)


def load_shares(amount, total, bound, lean, full):
    weights = [(1 << 20) // math.isqrt(rank ** lean) + 1 for rank in range(1, amount + 1)]
    largest = bound if full else min(bound, max(-(-total // amount), total * weights[0] // sum(weights)))
    least = 1 if total - largest >= amount - 1 else 0
    holding, rest = [largest] + [least] * (amount - 1), total - largest - least * (amount - 1)
    while rest > 0:
        movable = [i for i in range(1, amount) if holding[i] < largest] or [i for i in range(1, amount) if holding[i] < bound]
        mass, budget = sum([weights[i] for i in movable]), rest
        for i in movable:
            addition = min(bound - holding[i], max(1, budget * weights[i] // mass), rest)
            holding[i] = holding[i] + addition
            rest = rest - addition
    return np.array(holding)


def noise(stream_key, shape, width, most, cuts=(), held_as=jnp.bfloat16):
    gain = levels(stream_key, shape, cuts, -0.22, 0.18) if cuts else 1.0
    array = jax.random.normal(stream_key, shape, jnp.float32) * width * gain
    return jnp.minimum(jnp.maximum(array, -most), most).astype(held_as)


def setup_inputs(seed: int = 0, part: int = 0) -> dict:
    splits = jax.random.split(jax.random.key(seed), 12)
    own_keys = jax.random.split(jax.random.fold_in(splits[11], part), 12)
    queries = draw_queries(jax.random.fold_in(jax.random.fold_in(splits[11], part), 71), part)
    keys = draw_keys(jax.random.fold_in(jax.random.fold_in(splits[11], part), 71), part)
    values = noise(own_keys[2], (TOKENS, CTX, KVH * HDIM), 1.0, 6.0, ((0, 32),))
    kv_lengths = draw_kv_lengths(jax.random.fold_in(jax.random.fold_in(splits[11], part), 71), part)
    residual = noise(own_keys[4], (TOKENS, D), 1.0, 6.0, ((0, 32),))
    norm_gain = jnp.clip(1.0 + 0.1 * jax.random.normal(splits[5], (D,), jnp.float32), 0.5, 1.5).astype(jnp.bfloat16)
    routes_keys = jax.random.split(jax.random.fold_in(own_keys[6], 1), TOKENS // MB_ROWS)
    routes_turns = jax.random.permutation(jax.random.fold_in(own_keys[6], 3), TOKENS // MB_ROWS)
    routes = jax.vmap(lambda own, number: assign_block(jax.random.fold_in(own_keys[6], 2), own, number, MB_ROWS, EXPERTS, TOP, CAP, 2))(routes_keys, routes_turns).reshape((TOKENS, TOP))
    route_weights = jnp.clip(jnp.exp(math.log(0.5) - 1.6133518 * jax.random.uniform(own_keys[7], (TOKENS, TOP), jnp.float32) ** levels(own_keys[7], (TOKENS, TOP), ((0, 32),), -0.2, 0.2)), 0.099609375, 0.5).astype(jnp.bfloat16)
    gate_weight = noise(splits[8], (N_EP, D, HALF), D ** -0.5, 0.09375, ((0, 32),))
    up_weight = noise(splits[9], (N_EP, D, HALF), D ** -0.5, 0.09375, ((0, 32),))
    down_weight = noise(splits[10], (N_EP, HALF, D), HID ** -0.5, 0.21875, ((0, 32),))
    return {"queries": queries, "keys": keys, "values": values, "kv_lengths": kv_lengths, "residual": residual, "norm_gain": norm_gain, "routes": routes, "route_weights": route_weights, "gate_weight": gate_weight, "up_weight": up_weight, "down_weight": down_weight}


def attention_rows(query_rows, key_rows, value_rows, length_rows):
    row_count = query_rows.shape[0]
    positions = key_rows.shape[1]
    head_dim = key_rows.shape[2] // KVH
    query_heads = query_rows.reshape(row_count, KVH, -1, head_dim).astype(jnp.float32)
    key_heads = key_rows.reshape(row_count, positions, KVH, head_dim).astype(jnp.float32)
    value_heads = value_rows.reshape(row_count, positions, KVH, head_dim).astype(jnp.float32)
    scores = jnp.einsum('rgqd,rcgd->rgqc', query_heads, key_heads) * head_dim ** (-0.5)
    visible = jnp.arange(positions, dtype=jnp.int32)[None, :] < length_rows[:, None]
    scores = jnp.where(visible[:, None, None, :], scores, -1e+30)
    highest = lax.optimization_barrier(jnp.max(scores, axis=-1, keepdims=True))
    raw_weights = jnp.exp(scores - highest)
    weights = (raw_weights / lax.optimization_barrier(jnp.sum(raw_weights, axis=-1, keepdims=True))).astype(jnp.bfloat16)
    mixed_heads = jnp.einsum('rgqc,rcgd->rgqd', weights.astype(jnp.float32), value_heads)
    return mixed_heads.astype(jnp.bfloat16).reshape(row_count, -1)

def slot_tables(route_block, weight_block, experts, capacity):
    expert_ids = jnp.arange(experts, dtype=jnp.int32)
    onehot = (route_block[:, :, None] == expert_ids).astype(jnp.int32)
    chosen = lax.optimization_barrier(jnp.sum(onehot, axis=1))
    earlier = jnp.cumsum(chosen, axis=0) - chosen
    slot_rank = lax.optimization_barrier(jnp.sum(onehot * earlier[:, None, :], axis=2))
    target = route_block * capacity + slot_rank
    slot_ids = jnp.arange(experts * capacity, dtype=jnp.int32)
    slot_hits = target[:, :, None] == slot_ids
    select = lax.optimization_barrier(jnp.sum(slot_hits.astype(jnp.float32), axis=1)).astype(jnp.bfloat16)
    weighted = lax.optimization_barrier(jnp.sum(jnp.where(slot_hits, weight_block.astype(jnp.float32)[:, :, None], jnp.float32(0.0)), axis=1))
    return (select, weighted.astype(jnp.bfloat16))

def expert_block(rows_in, gate_full, up_full, down_full):
    gate_values = jnp.dot(rows_in, gate_full, preferred_element_type=jnp.float32)
    up_values = jnp.dot(rows_in, up_full, preferred_element_type=jnp.float32)
    hidden = (jax.nn.silu(gate_values) * up_values).astype(jnp.bfloat16)
    return jnp.dot(hidden, down_full, preferred_element_type=jnp.float32)

def reference(queries, keys, values, kv_lengths, residual, norm_gain, routes, route_weights, gate_weight, up_weight, down_weight):
    attended = attention_rows(queries, keys, values, kv_lengths)
    middle = residual.astype(jnp.float32) + attended.astype(jnp.float32)
    mean_square = lax.optimization_barrier(jnp.mean(middle * middle, axis=-1, keepdims=True))
    normed = (middle * lax.rsqrt(mean_square + 1e-06) * norm_gain.astype(jnp.float32)).astype(jnp.bfloat16)
    blocks = TOKENS // MB_ROWS
    route_blocks = routes.reshape(blocks, MB_ROWS, TOP)
    weight_blocks = route_weights.reshape(blocks, MB_ROWS, TOP)
    select, weighted = jax.vmap(lambda route_row, weight_row: slot_tables(route_row, weight_row, EXPERTS, CAP))(route_blocks, weight_blocks)
    gathered = jnp.einsum('bjm,bmd->bjd', jnp.swapaxes(select, 1, 2).astype(jnp.float32), normed.reshape(blocks, MB_ROWS, D).astype(jnp.float32)).astype(jnp.bfloat16)
    per_expert = gathered.reshape(blocks, EXPERTS, CAP, D).transpose(1, 0, 2, 3).reshape(EXPERTS, blocks * CAP, D)
    gate_full = gate_weight.reshape(EXPERTS, 2, D, HALF).transpose(0, 2, 1, 3).reshape(EXPERTS, D, HID)
    up_full = up_weight.reshape(EXPERTS, 2, D, HALF).transpose(0, 2, 1, 3).reshape(EXPERTS, D, HID)
    down_full = down_weight.reshape(EXPERTS, HID, D)
    outputs = lax.map(lambda expert_items: expert_block(*expert_items).astype(jnp.bfloat16), (per_expert, gate_full, up_full, down_full))
    returned = outputs.reshape(EXPERTS, blocks, CAP, D).transpose(1, 0, 2, 3).reshape(blocks, EXPERTS * CAP, D)
    combined = jnp.einsum('bmj,bjd->bmd', weighted.astype(jnp.float32), returned.astype(jnp.float32))
    return (middle + combined.reshape(TOKENS, D)).astype(jnp.bfloat16)
```

```python
import jax
import jax.numpy as jnp
from jax import lax
from jax.sharding import PartitionSpec as P

KVH = 2


def attention_rows(query_rows, key_rows, value_rows, length_rows):
    row_count = query_rows.shape[0]
    positions = key_rows.shape[1]
    head_dim = key_rows.shape[2] // KVH
    query_heads = query_rows.reshape(row_count, KVH, -1, head_dim)
    key_heads = key_rows.reshape(row_count, positions, KVH, head_dim)
    value_heads = value_rows.reshape(row_count, positions, KVH, head_dim)
    scores = jnp.einsum(
        "rgqd,rcgd->rgqc", query_heads, key_heads, preferred_element_type=jnp.float32
    ) * head_dim ** (-0.5)
    visible = jnp.arange(positions, dtype=jnp.int32)[None, :] < length_rows[:, None]
    scores = jnp.where(visible[:, None, None, :], scores, -1e30)
    highest = jnp.max(scores, axis=-1, keepdims=True)
    raw_weights = jnp.exp(scores - highest)
    weights = (raw_weights / jnp.sum(raw_weights, axis=-1, keepdims=True)).astype(jnp.bfloat16)
    mixed_heads = jnp.einsum(
        "rgqc,rcgd->rgqd", weights, value_heads, preferred_element_type=jnp.float32
    )
    return mixed_heads.astype(jnp.bfloat16).reshape(row_count, -1)


def local(
    queries,
    keys,
    values,
    kv_lengths,
    residual,
    norm_gain,
    routes,
    route_weights,
    gate_weight,
    up_weight,
    down_weight,
):
    devices = lax.axis_size("ep")
    experts = devices // 2
    width = residual.shape[1]
    lanes = -(-experts // 128) * 128
    mine = lax.axis_index("ep") // 2
    attended = attention_rows(queries, keys, values, kv_lengths)
    middle = residual.astype(jnp.float32) + attended.astype(jnp.float32)
    mean_square = jnp.mean(middle * middle, axis=-1, keepdims=True)
    normed = (middle * lax.rsqrt(mean_square + 1e-06) * norm_gain.astype(jnp.float32)).astype(
        jnp.bfloat16
    )
    hits = routes[:, :, None] == jnp.arange(lanes, dtype=jnp.int32)
    dense = jnp.sum(
        jnp.where(hits, route_weights.astype(jnp.float32)[:, :, None], 0.0), axis=1
    ).astype(jnp.bfloat16)
    packed = jnp.concatenate([normed, dense], axis=1)
    gathered = lax.all_gather(packed, "ep", axis=0, tiled=True)
    rows = gathered[:, :width]
    scale = jnp.sum(
        jnp.where(
            jnp.arange(lanes, dtype=jnp.int32)[None, :] == mine,
            gathered[:, width:].astype(jnp.float32),
            0.0,
        ),
        axis=1,
        keepdims=True,
    )
    gate_values = jnp.dot(rows, gate_weight[0], preferred_element_type=jnp.float32)
    up_values = jnp.dot(rows, up_weight[0], preferred_element_type=jnp.float32)
    hidden = (jax.nn.silu(gate_values) * up_values).astype(jnp.bfloat16)
    partial_out = jnp.dot(hidden, down_weight[0], preferred_element_type=jnp.float32)
    partial_out = (partial_out * scale).astype(jnp.bfloat16)
    combined = lax.psum_scatter(partial_out, "ep", scatter_dimension=0, tiled=True)
    return (middle + combined.astype(jnp.float32)).astype(jnp.bfloat16)


def solution(mesh):
    rows = P(("groups", "ep"), None)
    cache = P(("groups", "ep"), None, None)
    expert = P("ep", None, None)
    in_specs = (rows, cache, cache, P(("groups", "ep")), rows, P(), rows, rows, expert, expert, expert)
    return jax.shard_map(local, mesh=mesh, in_specs=in_specs, out_specs=rows, check_vma=False)
```

```python
import functools

import jax
import jax.numpy as jnp
from jax import lax
from jax.experimental import pallas as pl
from jax.experimental.pallas import tpu as pltpu
from jax.sharding import PartitionSpec as P

KVH = 2
VMEM_BUDGET = 40 << 20


def place(position, devices):
    quarter, rest = divmod(position, devices // 4)
    return (0, 2, 1, 3)[quarter] * (devices // 4) + rest


def exchange_kernel(
    devices, own_ref, gate_hbm, up_hbm, down_hbm, out_ref,
    rows, parts, landed, hidden, gate, up, down,
    load_sem, gather_send, gather_recv, reduce_send, reduce_recv,
):
    stages = devices.bit_length() - 1
    count, width = own_ref.shape[0], gate_hbm.shape[1]
    quarter = devices // 4
    me = lax.axis_index("ep")
    core = me % 2
    bits = [1 << b for b in range(stages - 1, 2, -1)] + [4 - 2 * core, 2 + 2 * core, 1]
    partners = [me + bit * (1 - 2 * ((me // bit) % 2)) for bit in bits]

    loads = [
        pltpu.make_async_copy(source.at[0], target, load_sem.at[i])
        for i, (source, target) in enumerate(((gate_hbm, gate), (up_hbm, up), (down_hbm, down)))
    ]
    for load in loads:
        load.start()
    rows[0] = own_ref[...]
    barrier = pltpu.get_barrier_semaphore()
    for partner in partners:
        pl.semaphore_signal(
            barrier, inc=1, device_id={"ep": partner}, device_id_type=pl.DeviceIdType.MESH
        )
    pl.semaphore_wait(barrier, stages)

    def gather(stage, position):
        index = (1 << stage) - 1 + position
        return pltpu.make_async_remote_copy(
            src_ref=rows.at[place(position, devices)],
            dst_ref=rows.at[place(position + (1 << stage), devices)],
            send_sem=gather_send.at[index],
            recv_sem=gather_recv.at[index],
            device_id={"ep": partners[stage]},
            device_id_type=pl.DeviceIdType.MESH,
        )

    def reduce(stage, position):
        index = (1 << stage) - 1 + position
        return pltpu.make_async_remote_copy(
            src_ref=parts.at[place(position + (1 << stage), devices)],
            dst_ref=landed.at[index],
            send_sem=reduce_send.at[index],
            recv_sem=reduce_recv.at[index],
            device_id={"ep": partners[stage]},
            device_id_type=pl.DeviceIdType.MESH,
        )

    def add(stage, position):
        reduce(stage, position).wait_recv()
        spot = place(position, devices)
        total = parts[spot].astype(jnp.float32) + landed[(1 << stage) - 1 + position].astype(
            jnp.float32
        )
        parts[spot] = total.astype(jnp.bfloat16)

    def project(half):
        first = half * (devices // 2)
        block = (devices // 2) * count
        step = 1024
        gates = jnp.zeros((block, gate.shape[1]), jnp.float32)
        ups = jnp.zeros((block, gate.shape[1]), jnp.float32)
        for start in range(0, width, step):
            part = rows[first : first + devices // 2, :, start : start + step].reshape(block, step)
            gates += jnp.dot(
                part, gate[start : start + step, :], preferred_element_type=jnp.float32
            )
            ups += jnp.dot(part, up[start : start + step, :], preferred_element_type=jnp.float32)
        hidden[half * block : (half + 1) * block, :] = (
            gates / (1.0 + jnp.exp(-gates)) * ups
        ).astype(jnp.bfloat16)

    def finish(position):
        first = place(position, devices)
        block = quarter * count
        table = rows[first : first + quarter, :, width:].reshape(block, -1).astype(jnp.float32)
        lanes = lax.broadcasted_iota(jnp.int32, table.shape, 1)
        scale = jnp.sum(jnp.where(lanes == me // 2, table, 0.0), axis=1, keepdims=True)
        units = hidden[first * count : (first + quarter) * count, :]
        step = 512
        for start in range(0, width, step):
            product = jnp.dot(
                units, down[:, start : start + step], preferred_element_type=jnp.float32
            )
            parts[first : first + quarter, :, start : start + step] = (
                (product * scale).astype(jnp.bfloat16).reshape(quarter, count, step)
            )

    top = stages - 1
    for stage in range(stages):
        gather(stage, 0).start()
    for stage in range(top - 1):
        for position in range(1 << stage):
            gather(stage, position).wait_recv()
            for later in range(stage + 1, stages):
                gather(later, position + (1 << stage)).start()
    for position in range(quarter):
        gather(top, position).wait_recv()
    for load in loads:
        load.wait()
    project(0)
    for position in range(quarter):
        gather(top - 1, position).wait_recv()
        gather(top, position + quarter).start()
    for position in range(quarter, 2 * quarter):
        gather(top, position).wait_recv()
    project(1)

    finish(3 * quarter)
    for position in range(2 * quarter - 1, quarter - 1, -1):
        reduce(top, position).start()
    finish(2 * quarter)
    for position in range(quarter - 1, -1, -1):
        reduce(top, position).start()
    finish(quarter)
    for position in range(quarter - 1, -1, -1):
        add(top, position + quarter)
        reduce(top - 1, position).start()
    finish(0)
    for position in range(quarter - 1, -1, -1):
        add(top, position)
    for stage in range(top - 1, 0, -1):
        upper = 1 << (stage - 1)
        for position in range(upper - 1, -1, -1):
            add(stage, position + upper)
            reduce(stage - 1, position).start()
        for position in range(upper - 1, -1, -1):
            add(stage, position)
    reduce(0, 0).wait_recv()
    out_ref[...] = parts[0].astype(jnp.float32) + landed[0].astype(jnp.float32)
    for stage in range(stages):
        for position in range(1 << stage):
            gather(stage, position).wait_send()
            reduce(stage, position).wait_send()


def exchange(packed, gate_weight, up_weight, down_weight, devices):
    count, lanes = packed.shape
    _, width, half = gate_weight.shape
    dma = pltpu.SemaphoreType.DMA
    return pl.pallas_call(
        functools.partial(exchange_kernel, devices),
        out_shape=jax.ShapeDtypeStruct((count, width), jnp.float32),
        in_specs=[pl.BlockSpec(memory_space=pltpu.VMEM)] + [pl.BlockSpec(memory_space=pl.ANY)] * 3,
        out_specs=pl.BlockSpec(memory_space=pltpu.VMEM),
        scratch_shapes=[
            pltpu.VMEM((devices, count, lanes), jnp.bfloat16),
            pltpu.VMEM((devices, count, width), jnp.bfloat16),
            pltpu.VMEM((devices - 1, count, width), jnp.bfloat16),
            pltpu.VMEM((devices * count, half), jnp.bfloat16),
            pltpu.VMEM((width, half), jnp.bfloat16),
            pltpu.VMEM((width, half), jnp.bfloat16),
            pltpu.VMEM((half, width), jnp.bfloat16),
            dma((3,)),
            dma((devices - 1,)),
            dma((devices - 1,)),
            dma((devices - 1,)),
            dma((devices - 1,)),
        ],
        compiler_params=pltpu.CompilerParams(
            collective_id=0, has_side_effects=True, vmem_limit_bytes=VMEM_BUDGET
        ),
    )(packed, gate_weight, up_weight, down_weight)


def attention_rows(query_rows, key_rows, value_rows, length_rows):
    row_count = query_rows.shape[0]
    positions = key_rows.shape[1]
    head_dim = key_rows.shape[2] // KVH
    query_heads = query_rows.reshape(row_count, KVH, -1, head_dim)
    key_heads = key_rows.reshape(row_count, positions, KVH, head_dim)
    value_heads = value_rows.reshape(row_count, positions, KVH, head_dim)
    scores = jnp.einsum(
        "rgqd,rcgd->rgqc", query_heads, key_heads, preferred_element_type=jnp.float32
    ) * head_dim ** (-0.5)
    visible = jnp.arange(positions, dtype=jnp.int32)[None, :] < length_rows[:, None]
    scores = jnp.where(visible[:, None, None, :], scores, -1e30)
    highest = jnp.max(scores, axis=-1, keepdims=True)
    raw_weights = jnp.exp(scores - highest)
    weights = (raw_weights / jnp.sum(raw_weights, axis=-1, keepdims=True)).astype(jnp.bfloat16)
    mixed_heads = jnp.einsum(
        "rgqc,rcgd->rgqd", weights, value_heads, preferred_element_type=jnp.float32
    )
    return mixed_heads.astype(jnp.bfloat16).reshape(row_count, -1)


def local(
    queries,
    keys,
    values,
    kv_lengths,
    residual,
    norm_gain,
    routes,
    route_weights,
    gate_weight,
    up_weight,
    down_weight,
):
    devices = lax.axis_size("ep")
    experts = devices // 2
    width = residual.shape[1]
    lanes = -(-experts // 128) * 128
    mine = lax.axis_index("ep") // 2
    attended = attention_rows(queries, keys, values, kv_lengths)
    middle = residual.astype(jnp.float32) + attended.astype(jnp.float32)
    mean_square = jnp.mean(middle * middle, axis=-1, keepdims=True)
    normed = (middle * lax.rsqrt(mean_square + 1e-06) * norm_gain.astype(jnp.float32)).astype(
        jnp.bfloat16
    )
    hits = routes[:, :, None] == jnp.arange(lanes, dtype=jnp.int32)
    dense = jnp.sum(
        jnp.where(hits, route_weights.astype(jnp.float32)[:, :, None], 0.0), axis=1
    ).astype(jnp.bfloat16)
    packed = jnp.concatenate([normed, dense], axis=1)
    held = 3 * devices * packed.size * 2 + 3 * gate_weight.size * 2
    if held <= VMEM_BUDGET * 3 // 4 and devices >= 8 and devices & (devices - 1) == 0:
        combined = exchange(packed, gate_weight, up_weight, down_weight, devices)
        return (middle + combined).astype(jnp.bfloat16)
    gathered = lax.all_gather(packed, "ep", axis=0, tiled=True)
    rows = gathered[:, :width]
    scale = jnp.sum(
        jnp.where(
            jnp.arange(lanes, dtype=jnp.int32)[None, :] == mine,
            gathered[:, width:].astype(jnp.float32),
            0.0,
        ),
        axis=1,
        keepdims=True,
    )
    gate_values = jnp.dot(rows, gate_weight[0], preferred_element_type=jnp.float32)
    up_values = jnp.dot(rows, up_weight[0], preferred_element_type=jnp.float32)
    hidden = (jax.nn.silu(gate_values) * up_values).astype(jnp.bfloat16)
    partial_out = jnp.dot(hidden, down_weight[0], preferred_element_type=jnp.float32)
    partial_out = (partial_out * scale).astype(jnp.bfloat16)
    combined = lax.psum_scatter(partial_out, "ep", scatter_dimension=0, tiled=True)
    return (middle + combined.astype(jnp.float32)).astype(jnp.bfloat16)


def solution(mesh):
    rows = P(("groups", "ep"), None)
    cache = P(("groups", "ep"), None, None)
    expert = P("ep", None, None)
    in_specs = (rows, cache, cache, P(("groups", "ep")), rows, P(), rows, rows, expert, expert, expert)
    return jax.shard_map(local, mesh=mesh, in_specs=in_specs, out_specs=rows, check_vma=False)
```

```python
import functools

import jax
import jax.numpy as jnp
from jax import lax
from jax.experimental import pallas as pl
from jax.experimental.pallas import tpu as pltpu
from jax.sharding import PartitionSpec as P

KVH = 2
VMEM_BUDGET = 62 << 20


def place(position, devices):
    quarter, rest = divmod(position, devices // 4)
    return (0, 2, 1, 3)[quarter] * (devices // 4) + rest


def swapped(position, devices):
    high, low = devices // 4, devices // 8
    first, second = position // high % 2, position // low % 2
    return position + (second - first) * (high - low)


def exchange_kernel(
    devices, own_ref, gate_hbm, up_hbm, down_hbm, out_ref,
    rows, parts, landed, hidden, first_weights, down,
    load_sem, gather_send, gather_recv, reduce_send, reduce_recv,
):
    stages = devices.bit_length() - 1
    count, width = own_ref.shape[0], gate_hbm.shape[1]
    half_units = gate_hbm.shape[2]
    quarter = devices // 4
    me = lax.axis_index("ep")
    core = me % 2
    bits = [1 << b for b in range(stages - 1, 2, -1)] + [4 - 2 * core, 2 + 2 * core, 1]
    partners = [me + bit * (1 - 2 * ((me // bit) % 2)) for bit in bits]

    loads = [
        pltpu.make_async_copy(source.at[0], target, load_sem.at[i])
        for i, (source, target) in enumerate(((gate_hbm, first_weights.at[:, :half_units]), (up_hbm, first_weights.at[:, half_units:]), (down_hbm, down)))
    ]
    for load in loads:
        load.start()
    rows[0] = own_ref[...]
    barrier = pltpu.get_barrier_semaphore()
    for partner in partners:
        pl.semaphore_signal(
            barrier, inc=1, device_id={"ep": partner}, device_id_type=pl.DeviceIdType.MESH
        )
    pl.semaphore_wait(barrier, stages)

    def gather(stage, position):
        index = (1 << stage) - 1 + position
        return pltpu.make_async_remote_copy(
            src_ref=rows.at[place(position, devices)],
            dst_ref=rows.at[place(position + (1 << stage), devices)],
            send_sem=gather_send.at[index],
            recv_sem=gather_recv.at[index],
            device_id={"ep": partners[stage]},
            device_id_type=pl.DeviceIdType.MESH,
        )

    back = partners[:-3] + [partners[-2], partners[-3], partners[-1]]

    def spot(position):
        return place(swapped(position, devices), devices)

    def reduce(stage, position):
        index = (1 << stage) - 1 + position
        return pltpu.make_async_remote_copy(
            src_ref=parts.at[spot(position + (1 << stage))],
            dst_ref=landed.at[index],
            send_sem=reduce_send.at[index],
            recv_sem=reduce_recv.at[index],
            device_id={"ep": back[stage]},
            device_id_type=pl.DeviceIdType.MESH,
        )

    def add(stage, position):
        reduce(stage, position).wait_recv()
        total = parts[spot(position)].astype(jnp.float32) + landed[
            (1 << stage) - 1 + position
        ].astype(jnp.float32)
        parts[spot(position)] = total.astype(jnp.bfloat16)

    def project(half):
        first = half * (devices // 2)
        block = (devices // 2) * count
        step = 1024
        both = jnp.zeros((block, 2 * half_units), jnp.float32)
        for start in range(0, width, step):
            part = rows[first : first + devices // 2, :, start : start + step].reshape(block, step)
            both += jnp.dot(
                part, first_weights[start : start + step, :], preferred_element_type=jnp.float32
            )
        gates, ups = both[:, :half_units], both[:, half_units:]
        hidden[half * block : (half + 1) * block, :] = (
            gates / (1.0 + jnp.exp(-gates)) * ups
        ).astype(jnp.bfloat16)

    def finish(position):
        first = place(position, devices)
        block = quarter * count
        table = rows[first : first + quarter, :, width:].reshape(block, -1).astype(jnp.float32)
        lanes = lax.broadcasted_iota(jnp.int32, table.shape, 1)
        scale = jnp.sum(jnp.where(lanes == me // 2, table, 0.0), axis=1, keepdims=True)
        units = hidden[first * count : (first + quarter) * count, :]
        step = 512
        for start in range(0, width, step):
            product = jnp.dot(
                units, down[:, start : start + step], preferred_element_type=jnp.float32
            )
            parts[first : first + quarter, :, start : start + step] = (
                (product * scale).astype(jnp.bfloat16).reshape(quarter, count, step)
            )

    top = stages - 1
    for stage in range(stages):
        gather(stage, 0).start()
    for stage in range(top - 1):
        for position in range(1 << stage):
            gather(stage, position).wait_recv()
            for later in range(stage + 1, stages):
                gather(later, position + (1 << stage)).start()
    for position in range(quarter):
        gather(top, position).wait_recv()
    for load in loads:
        load.wait()
    eighth = quarter // 2
    early = [*range(quarter + eighth - 1, quarter - 1, -1), *range(eighth - 1, -1, -1)]
    late = [position + eighth for position in early]
    project(0)
    finish(2 * quarter)
    for position in early:
        reduce(top, position).start()
    for position in range(eighth):
        gather(top - 1, position).wait_recv()
        gather(top, position + quarter).start()
    finish(0)
    for position in range(eighth, quarter):
        gather(top - 1, position).wait_recv()
        gather(top, position + quarter).start()
    for position in early[:eighth]:
        add(top, position)
        reduce(top - 1, position - quarter).start()
    for position in range(quarter, 2 * quarter):
        gather(top, position).wait_recv()
    project(1)
    finish(3 * quarter)
    for position in late:
        reduce(top, position).start()
    finish(quarter)
    for position in late[:eighth]:
        add(top, position)
        reduce(top - 1, position - quarter).start()
    for position in late[eighth:] + early[eighth:]:
        add(top, position)
    for stage in range(top - 1, 0, -1):
        upper = 1 << (stage - 1)
        for position in range(upper - 1, -1, -1):
            add(stage, position + upper)
            reduce(stage - 1, position).start()
        for position in range(upper - 1, -1, -1):
            add(stage, position)
    reduce(0, 0).wait_recv()
    out_ref[...] = parts[0].astype(jnp.float32) + landed[0].astype(jnp.float32)
    for stage in range(stages):
        for position in range(1 << stage):
            gather(stage, position).wait_send()
            reduce(stage, position).wait_send()


def exchange(packed, gate_weight, up_weight, down_weight, devices):
    count, lanes = packed.shape
    _, width, half = gate_weight.shape
    dma = pltpu.SemaphoreType.DMA
    return pl.pallas_call(
        functools.partial(exchange_kernel, devices),
        out_shape=jax.ShapeDtypeStruct((count, width), jnp.float32),
        in_specs=[pl.BlockSpec(memory_space=pltpu.VMEM)] + [pl.BlockSpec(memory_space=pltpu.HBM)] * 3,
        out_specs=pl.BlockSpec(memory_space=pltpu.VMEM),
        scratch_shapes=[
            pltpu.VMEM((devices, count, lanes), jnp.bfloat16),
            pltpu.VMEM((devices, count, width), jnp.bfloat16),
            pltpu.VMEM((devices - 1, count, width), jnp.bfloat16),
            pltpu.VMEM((devices * count, half), jnp.bfloat16),
            pltpu.VMEM((width, 2 * half), jnp.bfloat16),
            pltpu.VMEM((half, width), jnp.bfloat16),
            dma((3,)),
            dma((devices - 1,)),
            dma((devices - 1,)),
            dma((devices - 1,)),
            dma((devices - 1,)),
        ],
        compiler_params=pltpu.CompilerParams(
            collective_id=0, has_side_effects=True, vmem_limit_bytes=VMEM_BUDGET
        ),
    )(packed, gate_weight, up_weight, down_weight)


def attention_rows(query_rows, key_rows, value_rows, length_rows):
    row_count = query_rows.shape[0]
    positions = key_rows.shape[1]
    head_dim = key_rows.shape[2] // KVH
    query_heads = query_rows.reshape(row_count, KVH, -1, head_dim)
    key_heads = key_rows.reshape(row_count, positions, KVH, head_dim)
    value_heads = value_rows.reshape(row_count, positions, KVH, head_dim)
    scores = jnp.einsum(
        "rgqd,rcgd->rgqc", query_heads, key_heads, preferred_element_type=jnp.float32
    ) * head_dim ** (-0.5)
    visible = jnp.arange(positions, dtype=jnp.int32)[None, :] < length_rows[:, None]
    scores = jnp.where(visible[:, None, None, :], scores, -1e30)
    highest = jnp.max(scores, axis=-1, keepdims=True)
    raw_weights = jnp.exp(scores - highest)
    weights = (raw_weights / jnp.sum(raw_weights, axis=-1, keepdims=True)).astype(jnp.bfloat16)
    mixed_heads = jnp.einsum(
        "rgqc,rcgd->rgqd", weights, value_heads, preferred_element_type=jnp.float32
    )
    return mixed_heads.astype(jnp.bfloat16).reshape(row_count, -1)


def local(
    queries,
    keys,
    values,
    kv_lengths,
    residual,
    norm_gain,
    routes,
    route_weights,
    gate_weight,
    up_weight,
    down_weight,
):
    devices = lax.axis_size("ep")
    experts = devices // 2
    width = residual.shape[1]
    lanes = -(-experts // 128) * 128
    mine = lax.axis_index("ep") // 2
    attended = attention_rows(queries, keys, values, kv_lengths)
    middle = residual.astype(jnp.float32) + attended.astype(jnp.float32)
    mean_square = jnp.mean(middle * middle, axis=-1, keepdims=True)
    normed = (middle * lax.rsqrt(mean_square + 1e-06) * norm_gain.astype(jnp.float32)).astype(
        jnp.bfloat16
    )
    hits = routes[:, :, None] == jnp.arange(lanes, dtype=jnp.int32)
    dense = jnp.sum(
        jnp.where(hits, route_weights.astype(jnp.float32)[:, :, None], 0.0), axis=1
    ).astype(jnp.bfloat16)
    packed = jnp.concatenate([normed, dense], axis=1)
    held = 3 * devices * packed.size * 2 + 3 * gate_weight.size * 2
    if held <= VMEM_BUDGET * 3 // 4 and devices >= 8 and devices & (devices - 1) == 0:
        combined = exchange(packed, gate_weight, up_weight, down_weight, devices)
        return (middle + combined).astype(jnp.bfloat16)
    gathered = lax.all_gather(packed, "ep", axis=0, tiled=True)
    rows = gathered[:, :width]
    scale = jnp.sum(
        jnp.where(
            jnp.arange(lanes, dtype=jnp.int32)[None, :] == mine,
            gathered[:, width:].astype(jnp.float32),
            0.0,
        ),
        axis=1,
        keepdims=True,
    )
    gate_values = jnp.dot(rows, gate_weight[0], preferred_element_type=jnp.float32)
    up_values = jnp.dot(rows, up_weight[0], preferred_element_type=jnp.float32)
    hidden = (jax.nn.silu(gate_values) * up_values).astype(jnp.bfloat16)
    partial_out = jnp.dot(hidden, down_weight[0], preferred_element_type=jnp.float32)
    partial_out = (partial_out * scale).astype(jnp.bfloat16)
    combined = lax.psum_scatter(partial_out, "ep", scatter_dimension=0, tiled=True)
    return (middle + combined.astype(jnp.float32)).astype(jnp.bfloat16)


def solution(mesh):
    rows = P(("groups", "ep"), None)
    cache = P(("groups", "ep"), None, None)
    expert = P("ep", None, None)
    in_specs = (rows, cache, cache, P(("groups", "ep")), rows, P(), rows, rows, expert, expert, expert)
    return jax.shard_map(local, mesh=mesh, in_specs=in_specs, out_specs=rows, check_vma=False)
```

```python
import functools

import jax
import jax.numpy as jnp
from jax import lax
from jax.experimental import pallas as pl
from jax.experimental.pallas import tpu as pltpu
from jax.sharding import PartitionSpec as P

KVH = 2
VMEM_BUDGET = 62 << 20


def place(position, devices):
    quarter, rest = divmod(position, devices // 4)
    return (0, 2, 1, 3)[quarter] * (devices // 4) + rest


def swapped(position, devices):
    high, low = devices // 4, devices // 8
    first, second = position // high % 2, position // low % 2
    return position + (second - first) * (high - low)


def exchange_kernel(
    devices, own_ref, gate_hbm, up_hbm, down_hbm, out_ref,
    rows, parts, landed, hidden, first_weights, down,
    load_sem, gather_send, gather_recv, reduce_send, reduce_recv,
):
    stages = devices.bit_length() - 1
    count, width = own_ref.shape[0], gate_hbm.shape[1]
    half_units = gate_hbm.shape[2]
    quarter = devices // 4
    me = lax.axis_index("ep")
    core = me % 2
    bits = [1 << b for b in range(stages - 1, 2, -1)] + [4 - 2 * core, 2 + 2 * core, 1]
    partners = [me + bit * (1 - 2 * ((me // bit) % 2)) for bit in bits]

    loads = [
        pltpu.make_async_copy(source.at[0], target, load_sem.at[i])
        for i, (source, target) in enumerate(((gate_hbm, first_weights.at[:, :half_units]), (up_hbm, first_weights.at[:, half_units:]), (down_hbm, down)))
    ]
    for load in loads:
        load.start()
    rows[0] = own_ref[...]
    barrier = pltpu.get_barrier_semaphore()
    for partner in partners:
        pl.semaphore_signal(
            barrier, inc=1, device_id={"ep": partner}, device_id_type=pl.DeviceIdType.MESH
        )
    pl.semaphore_wait(barrier, stages)

    def gather(stage, position):
        index = (1 << stage) - 1 + position
        return pltpu.make_async_remote_copy(
            src_ref=rows.at[place(position, devices)],
            dst_ref=rows.at[place(position + (1 << stage), devices)],
            send_sem=gather_send.at[index],
            recv_sem=gather_recv.at[index],
            device_id={"ep": partners[stage]},
            device_id_type=pl.DeviceIdType.MESH,
        )

    back = partners[:-3] + [partners[-2], partners[-3], partners[-1]]

    def spot(position):
        return place(swapped(position, devices), devices)

    def reduce(stage, position):
        index = (1 << stage) - 1 + position
        return pltpu.make_async_remote_copy(
            src_ref=parts.at[spot(position + (1 << stage))],
            dst_ref=landed.at[index],
            send_sem=reduce_send.at[index],
            recv_sem=reduce_recv.at[index],
            device_id={"ep": back[stage]},
            device_id_type=pl.DeviceIdType.MESH,
        )

    def add(stage, position):
        reduce(stage, position).wait_recv()
        total = parts[spot(position)].astype(jnp.float32) + landed[
            (1 << stage) - 1 + position
        ].astype(jnp.float32)
        parts[spot(position)] = total.astype(jnp.bfloat16)

    def project(first, taken):
        block = taken * count
        step = 1024
        both = jnp.zeros((block, 2 * half_units), jnp.float32)
        for start in range(0, width, step):
            part = rows[first : first + taken, :, start : start + step].reshape(block, step)
            both += jnp.dot(
                part, first_weights[start : start + step, :], preferred_element_type=jnp.float32
            )
        gates, ups = both[:, :half_units], both[:, half_units:]
        hidden[first * count : first * count + block, :] = (
            gates / (1.0 + jnp.exp(-gates)) * ups
        ).astype(jnp.bfloat16)

    def finish(position):
        first = place(position, devices)
        block = quarter * count
        table = rows[first : first + quarter, :, width:].reshape(block, -1).astype(jnp.float32)
        lanes = lax.broadcasted_iota(jnp.int32, table.shape, 1)
        scale = jnp.sum(jnp.where(lanes == me // 2, table, 0.0), axis=1, keepdims=True)
        units = hidden[first * count : (first + quarter) * count, :]
        step = 512
        for start in range(0, width, step):
            product = jnp.dot(
                units, down[:, start : start + step], preferred_element_type=jnp.float32
            )
            parts[first : first + quarter, :, start : start + step] = (
                (product * scale).astype(jnp.bfloat16).reshape(quarter, count, step)
            )

    top = stages - 1
    for stage in range(stages):
        gather(stage, 0).start()
    for stage in range(top - 1):
        for position in range(1 << stage):
            gather(stage, position).wait_recv()
            for later in range(stage + 1, stages):
                gather(later, position + (1 << stage)).start()
    for load in loads:
        load.wait()
    eighth = quarter // 2
    early = [*range(quarter + eighth - 1, quarter - 1, -1), *range(eighth - 1, -1, -1)]
    late = [position + eighth for position in early]
    project(0, quarter)
    for position in range(quarter):
        gather(top, position).wait_recv()
    project(quarter, quarter)
    finish(2 * quarter)
    for position in early:
        reduce(top, position).start()
    for position in range(eighth):
        gather(top - 1, position).wait_recv()
        gather(top, position + quarter).start()
    finish(0)
    for position in range(eighth, quarter):
        gather(top - 1, position).wait_recv()
        gather(top, position + quarter).start()
    for position in early[:eighth]:
        add(top, position)
        reduce(top - 1, position - quarter).start()
    for position in early[eighth:]:
        add(top, position)
    project(2 * quarter, quarter)
    finish(quarter)
    for position in range(quarter, 2 * quarter):
        gather(top, position).wait_recv()
    project(3 * quarter, quarter)
    finish(3 * quarter)
    for position in late:
        reduce(top, position).start()
    for position in late[:eighth]:
        add(top, position)
        reduce(top - 1, position - quarter).start()
    for position in late[eighth:]:
        add(top, position)
    for stage in range(top - 1, 0, -1):
        upper = 1 << (stage - 1)
        for position in range(upper - 1, -1, -1):
            add(stage, position + upper)
            reduce(stage - 1, position).start()
        for position in range(upper - 1, -1, -1):
            add(stage, position)
    reduce(0, 0).wait_recv()
    out_ref[...] = parts[0].astype(jnp.float32) + landed[0].astype(jnp.float32)
    for stage in range(stages):
        for position in range(1 << stage):
            gather(stage, position).wait_send()
            reduce(stage, position).wait_send()


def exchange(packed, gate_weight, up_weight, down_weight, devices):
    count, lanes = packed.shape
    _, width, half = gate_weight.shape
    dma = pltpu.SemaphoreType.DMA
    return pl.pallas_call(
        functools.partial(exchange_kernel, devices),
        out_shape=jax.ShapeDtypeStruct((count, width), jnp.float32),
        in_specs=[pl.BlockSpec(memory_space=pltpu.VMEM)] + [pl.BlockSpec(memory_space=pltpu.HBM)] * 3,
        out_specs=pl.BlockSpec(memory_space=pltpu.VMEM),
        scratch_shapes=[
            pltpu.VMEM((devices, count, lanes), jnp.bfloat16),
            pltpu.VMEM((devices, count, width), jnp.bfloat16),
            pltpu.VMEM((devices - 1, count, width), jnp.bfloat16),
            pltpu.VMEM((devices * count, half), jnp.bfloat16),
            pltpu.VMEM((width, 2 * half), jnp.bfloat16),
            pltpu.VMEM((half, width), jnp.bfloat16),
            dma((3,)),
            dma((devices - 1,)),
            dma((devices - 1,)),
            dma((devices - 1,)),
            dma((devices - 1,)),
        ],
        compiler_params=pltpu.CompilerParams(
            collective_id=0, has_side_effects=True, vmem_limit_bytes=VMEM_BUDGET
        ),
    )(packed, gate_weight, up_weight, down_weight)


def attention_rows(query_rows, key_rows, value_rows, length_rows):
    row_count = query_rows.shape[0]
    positions = key_rows.shape[1]
    head_dim = key_rows.shape[2] // KVH
    query_heads = query_rows.reshape(row_count, KVH, -1, head_dim)
    key_heads = key_rows.reshape(row_count, positions, KVH, head_dim)
    value_heads = value_rows.reshape(row_count, positions, KVH, head_dim)
    scores = jnp.einsum(
        "rgqd,rcgd->rgqc", query_heads, key_heads, preferred_element_type=jnp.float32
    ) * head_dim ** (-0.5)
    visible = jnp.arange(positions, dtype=jnp.int32)[None, :] < length_rows[:, None]
    scores = jnp.where(visible[:, None, None, :], scores, -1e30)
    highest = jnp.max(scores, axis=-1, keepdims=True)
    raw_weights = jnp.exp(scores - highest)
    weights = (raw_weights / jnp.sum(raw_weights, axis=-1, keepdims=True)).astype(jnp.bfloat16)
    mixed_heads = jnp.einsum(
        "rgqc,rcgd->rgqd", weights, value_heads, preferred_element_type=jnp.float32
    )
    return mixed_heads.astype(jnp.bfloat16).reshape(row_count, -1)


def local(
    queries,
    keys,
    values,
    kv_lengths,
    residual,
    norm_gain,
    routes,
    route_weights,
    gate_weight,
    up_weight,
    down_weight,
):
    devices = lax.axis_size("ep")
    experts = devices // 2
    width = residual.shape[1]
    lanes = -(-experts // 128) * 128
    mine = lax.axis_index("ep") // 2
    attended = attention_rows(queries, keys, values, kv_lengths)
    middle = residual.astype(jnp.float32) + attended.astype(jnp.float32)
    mean_square = jnp.mean(middle * middle, axis=-1, keepdims=True)
    normed = (middle * lax.rsqrt(mean_square + 1e-06) * norm_gain.astype(jnp.float32)).astype(
        jnp.bfloat16
    )
    hits = routes[:, :, None] == jnp.arange(lanes, dtype=jnp.int32)
    dense = jnp.sum(
        jnp.where(hits, route_weights.astype(jnp.float32)[:, :, None], 0.0), axis=1
    ).astype(jnp.bfloat16)
    packed = jnp.concatenate([normed, dense], axis=1)
    held = 3 * devices * packed.size * 2 + 3 * gate_weight.size * 2
    if held <= VMEM_BUDGET * 3 // 4 and devices >= 8 and devices & (devices - 1) == 0:
        combined = exchange(packed, gate_weight, up_weight, down_weight, devices)
        return (middle + combined).astype(jnp.bfloat16)
    gathered = lax.all_gather(packed, "ep", axis=0, tiled=True)
    rows = gathered[:, :width]
    scale = jnp.sum(
        jnp.where(
            jnp.arange(lanes, dtype=jnp.int32)[None, :] == mine,
            gathered[:, width:].astype(jnp.float32),
            0.0,
        ),
        axis=1,
        keepdims=True,
    )
    gate_values = jnp.dot(rows, gate_weight[0], preferred_element_type=jnp.float32)
    up_values = jnp.dot(rows, up_weight[0], preferred_element_type=jnp.float32)
    hidden = (jax.nn.silu(gate_values) * up_values).astype(jnp.bfloat16)
    partial_out = jnp.dot(hidden, down_weight[0], preferred_element_type=jnp.float32)
    partial_out = (partial_out * scale).astype(jnp.bfloat16)
    combined = lax.psum_scatter(partial_out, "ep", scatter_dimension=0, tiled=True)
    return (middle + combined.astype(jnp.float32)).astype(jnp.bfloat16)


def solution(mesh):
    rows = P(("groups", "ep"), None)
    cache = P(("groups", "ep"), None, None)
    expert = P("ep", None, None)
    in_specs = (rows, cache, cache, P(("groups", "ep")), rows, P(), rows, rows, expert, expert, expert)
    return jax.shard_map(local, mesh=mesh, in_specs=in_specs, out_specs=rows, check_vma=False)
```
